32 devices in a mesh: tensor: 4 (over y, core), dp: 8 (over z, x).
Axes of the slice: x: 2, y: 2, z: 4, core: 2. Of those that a mesh axis runs over, the one named last changes fastest.
Arguments:
- inputs: bfloat16 [4096, 512], P('dp'), may hold values from -6 to 6
- norm_gains: bfloat16 [5, 512], replicated, may hold values from 0.25 to 1.75
- early_up: bfloat16 [512, 2048], P(None, 'tensor'), may hold values from -0.25 to 0.25
- early_down: bfloat16 [2048, 512], P('tensor'), may hold values from -0.25 to 0.25
- query_key_value: bfloat16 [512, 3, 512], P(None, None, 'tensor'), may hold values from -0.25 to 0.25
- position_weight: bfloat16 [512, 512], P(None, 'tensor'), may hold values from -0.25 to 0.25
- position_bias: bfloat16 [2, 8, 64], P(None, 'tensor'), may hold values from -3 to 3
- attention_out: bfloat16 [512, 512], P('tensor'), may hold values from -0.75 to 0.75
- pointwise_in: bfloat16 [512, 2, 512], P(None, None, 'tensor'), may hold values from -0.25 to 0.25
- depthwise: bfloat16 [31, 512], P(None, 'tensor'), may hold values from -1 to 1
- batch_gain: bfloat16 [512], P('tensor'), may hold values from 0.25 to 1.75
- batch_bias: bfloat16 [512], P('tensor'), may hold values from -3 to 3
- pointwise_out: bfloat16 [512, 512], P('tensor'), may hold values from -0.375 to 0.375
- late_up: bfloat16 [512, 2048], P(None, 'tensor'), may hold values from -0.25 to 0.25
- late_down: bfloat16 [2048, 512], P('tensor'), may hold values from -0.25 to 0.25
- output_cotangent: bfloat16 [4096, 512], P('dp'), may hold values from -6 to 6
Outputs:
- layer_output: bfloat16 [4096, 512], P('dp')
- input_gradient: float32 [4096, 512], P('dp')
- gains_gradient: float32 [5, 512], replicated
- early_up_gradient: float32 [512, 2048], P(None, 'tensor')
- early_down_gradient: float32 [2048, 512], P('tensor')
- query_key_value_gradient: float32 [512, 3, 512], P(None, None, 'tensor')
- position_weight_gradient: float32 [512, 512], P(None, 'tensor')
- position_bias_gradient: float32 [2, 8, 64], P(None, 'tensor')
- attention_out_gradient: float32 [512, 512], P('tensor')
- pointwise_in_gradient: float32 [512, 2, 512], P(None, None, 'tensor')
- depthwise_gradient: float32 [31, 512], P(None, 'tensor')
- batch_gain_gradient: float32 [512], P('tensor')
- batch_bias_gradient: float32 [512], P('tensor')
- pointwise_out_gradient: float32 [512, 512], P('tensor')
- late_up_gradient: float32 [512, 2048], P(None, 'tensor')
- late_down_gradient: float32 [2048, 512], P('tensor')
The draws below stay inside these ranges and needn't reach their ends.
All inputs are finite; a program needn't handle non-finite values.
Results may differ from the reference program's by a relative error of at most 0.02.
Values sent between devices are 32-bit elements; how exact they have to be, the bound alone decides.
A program may use at most 128 MiB of HBM per device.

```python
import math
import jax
import jax.numpy as jnp
from jax import lax

D = 512
HEADS = 8
HEAD_SIZE = 64
FF = 2048
KERNEL = 31
LENGTH = 512
TOKENS = 4096


def level_of(rng, extent, shards, smallest, largest):
    level = 1.0
    for axis_at, blocks in shards:
        steps = jax.random.uniform(jax.random.fold_in(jax.random.fold_in(rng, 6), axis_at), (blocks,), jnp.float32, smallest / len(shards), largest / len(shards))
        level = level * jnp.repeat(jnp.exp(steps), extent[axis_at] // blocks).reshape((-1,) + (1,) * (len(extent) - 1 - axis_at))
    return level


def normal_values(rng, shape, scale, reach, split=(), kind=jnp.bfloat16):
    entries = scale * jax.random.normal(rng, shape, jnp.float32)
    if split:
        entries = entries * level_of(rng, shape, split, -0.22, 0.18)
    return jnp.clip(entries, -reach, reach).astype(kind)


def setup_inputs(seed: int = 0) -> dict:
    seeds = jax.random.split(jax.random.key(seed), 17)
    return {
        "inputs": normal_values(seeds[0], (TOKENS, D), 1.0, 6.0, ((0, 8),)),
        "norm_gains": jnp.clip(1.0 + 0.15 * jax.random.normal(seeds[1], (5, D), jnp.float32), 0.25, 1.75).astype(jnp.bfloat16),
        "early_up": normal_values(seeds[2], (D, FF), D ** -0.5, 0.25, ((1, 4),)),
        "early_down": normal_values(seeds[3], (FF, D), (FF // 4) ** -0.5, 0.25, ((0, 4),)),
        "query_key_value": normal_values(seeds[4], (D, 3, D), D ** -0.5, 0.25, ((2, 4),)),
        "position_weight": normal_values(seeds[5], (D, D), D ** -0.5, 0.25, ((1, 4),)),
        "position_bias": normal_values(seeds[6], (2, HEADS, HEAD_SIZE), 0.5, 3.0, ((1, 4),)),
        "attention_out": normal_values(seeds[7], (D, D), (D // 8) ** -0.5, 0.75, ((0, 4),)),
        "pointwise_in": normal_values(seeds[8], (D, 2, D), D ** -0.5, 0.25, ((2, 4),)),
        "depthwise": normal_values(seeds[9], (KERNEL, D), KERNEL ** -0.5, 1.0, ((1, 4),)),
        "batch_gain": jnp.clip(1.0 + 0.15 * jax.random.normal(seeds[10], (D,), jnp.float32), 0.25, 1.75).astype(jnp.bfloat16),
        "batch_bias": normal_values(seeds[11], (D,), 0.5, 3.0, ((0, 4),)),
        "pointwise_out": normal_values(seeds[12], (D, D), (D // 2) ** -0.5, 0.375, ((0, 4),)),
        "late_up": normal_values(seeds[13], (D, FF), D ** -0.5, 0.25, ((1, 4),)),
        "late_down": normal_values(seeds[14], (FF, D), (FF // 4) ** -0.5, 0.25, ((0, 4),)),
        "output_cotangent": normal_values(seeds[15], (TOKENS, D), 1.0, 6.0, ((0, 8),)),
    }


EPS = 1e-05
HIGH = lax.Precision.HIGHEST

@jax.custom_vjp
def low(v):
    return lax.optimization_barrier(v.astype(jnp.bfloat16)).astype(jnp.float32)

@jax.custom_vjp
def low_back(v):
    return v

def low_keep(v):
    return (low(v), None)

def low_pass(kept, grad):
    return (grad,)

def back_keep(v):
    return (v, None)

def back_low(kept, grad):
    return (low(grad),)
low.defvjp(low_keep, low_pass)
low_back.defvjp(back_keep, back_low)

def matmul(first_factor, second_factor):
    return jnp.dot(first_factor, second_factor, precision=HIGH, preferred_element_type=jnp.float32)

def layer_norm(values, gain_row):
    centre = values - lax.optimization_barrier(jnp.mean(values, axis=-1, keepdims=True))
    spread = lax.optimization_barrier(jnp.mean(centre * centre, axis=-1, keepdims=True))
    return centre * lax.rsqrt(spread + EPS) * gain_row

def sinusoid_table(length, model_width):
    offsets = (length - 1 - jnp.arange(2 * length - 1)).astype(jnp.float32)
    frequency = jnp.exp(jnp.arange(0, model_width, 2).astype(jnp.float32) * (-math.log(10000.0) / model_width))
    phases = offsets[:, None] * frequency[None, :]
    return jnp.stack([jnp.sin(phases), jnp.cos(phases)], axis=-1).reshape(2 * length - 1, model_width)

def relative_shift(scores):
    head_count, length, span_size = scores.shape
    padded = jnp.pad(scores, ((0, 0), (0, 0), (1, 0)))
    padded = padded.reshape(head_count, 2 * length, length)[:, 1:]
    return padded.reshape(head_count, length, span_size)[:, :, :length]

def feed_forward(values, gain_row, weight_in, weight_out):
    normed = low(layer_norm(values, gain_row))
    hidden = low_back(matmul(normed, weight_in))
    active = low(jax.nn.silu(hidden))
    return low_back(matmul(active, weight_out))

def sequence_core(sequence, sinusoid, weight_pos, biases):
    length = sequence.shape[0]
    head_count = sequence.shape[2]
    head_size = sequence.shape[3]
    queries = sequence[:, 0]
    key_rows = low(sequence[:, 1])
    values = low(sequence[:, 2])
    position = low(low_back(matmul(sinusoid, weight_pos))).reshape(2 * length - 1, head_count, head_size)
    with_content = low(queries + biases[0])
    with_position = low(queries + biases[1])
    content = jnp.einsum('ihd,jhd->hij', with_content, key_rows, precision=HIGH, preferred_element_type=jnp.float32)
    relative = relative_shift(jnp.einsum('ihd,rhd->hir', with_position, position, precision=HIGH, preferred_element_type=jnp.float32))
    scores = low_back((content + relative) * (1.0 / math.sqrt(head_size)))
    weights = low(jax.nn.softmax(scores, axis=-1))
    return jnp.einsum('hij,jhd->ihd', weights, values, precision=HIGH, preferred_element_type=jnp.float32)

def attention(values, gain_row, weight_qkv, weight_pos, biases, weight_out):
    model_width = weight_qkv.shape[0]
    local_width = weight_qkv.shape[2]
    head_count = biases.shape[1]
    head_size = biases.shape[2]
    normed = low(layer_norm(values, gain_row))
    mixed_rows = low_back(matmul(normed, weight_qkv.reshape(model_width, 3 * local_width)))
    mixed_rows = mixed_rows.reshape(-1, LENGTH, 3, head_count, head_size)
    sinusoid = low(sinusoid_table(LENGTH, model_width))
    per_sequence = jax.checkpoint(lambda sequence: sequence_core(sequence, sinusoid, weight_pos, biases))
    attended = lax.map(per_sequence, mixed_rows).reshape(-1, local_width)
    attended = low(low_back(attended))
    return low_back(matmul(attended, weight_out))

def depthwise_conv(gated, kernel):
    half = kernel.shape[0] // 2
    return lax.conv_general_dilated(gated, kernel[:, None, :], (1,), [(half, half)], dimension_numbers=('NWC', 'WIO', 'NWC'), feature_group_count=gated.shape[2], precision=HIGH)

def conv_front(values, gain_row, weight_in, kernel):
    channels = kernel.shape[1]
    normed = low(layer_norm(values, gain_row))
    paired = low_back(matmul(normed, weight_in.reshape(weight_in.shape[0], 2 * channels))).reshape(-1, 2, channels)
    gated = paired[:, 0] * jax.nn.sigmoid(paired[:, 1])
    return depthwise_conv(gated.reshape(-1, LENGTH, channels), kernel)

def conv_back(mixed_rows, batch_mean, batch_var, scale_row, shift_row, weight_out):
    scaled = (mixed_rows - batch_mean) * lax.rsqrt(batch_var + EPS) * scale_row + shift_row
    swished = low(jax.nn.silu(scaled)).reshape(-1, mixed_rows.shape[2])
    return low_back(matmul(swished, weight_out))

def forward(inputs, norm_gains, early_up, early_down, query_key_value, position_weight, position_bias, attention_out, pointwise_in, depthwise, batch_gain, batch_bias, pointwise_out, late_up, late_down):
    after_first = inputs + 0.5 * feed_forward(inputs, norm_gains[0], early_up, early_down)
    after_second = after_first + attention(after_first, norm_gains[1], query_key_value, position_weight, position_bias, attention_out)
    mixed_rows = conv_front(after_second, norm_gains[2], pointwise_in, depthwise)
    batch_mean = lax.optimization_barrier(jnp.mean(mixed_rows, axis=(0, 1)))
    batch_var = lax.optimization_barrier(jnp.mean((mixed_rows - batch_mean) ** 2, axis=(0, 1)))
    after_third = after_second + conv_back(mixed_rows, batch_mean, batch_var, batch_gain, batch_bias, pointwise_out)
    after_fourth = after_third + 0.5 * feed_forward(after_third, norm_gains[3], late_up, late_down)
    return layer_norm(after_fourth, norm_gains[4])

def reference(inputs, norm_gains, early_up, early_down, query_key_value, position_weight, position_bias, attention_out, pointwise_in, depthwise, batch_gain, batch_bias, pointwise_out, late_up, late_down, output_cotangent):
    arrays = [item.astype(jnp.float32) for item in (inputs, norm_gains, early_up, early_down, query_key_value, position_weight, position_bias, attention_out, pointwise_in, depthwise, batch_gain, batch_bias, pointwise_out, late_up, late_down)]
    result, pullback = jax.vjp(forward, *arrays)
    grads = pullback(output_cotangent.astype(jnp.float32))
    return (result.astype(jnp.bfloat16), grads[0], grads[1], grads[2], grads[3], grads[4], grads[5], grads[6], grads[7], grads[8], grads[9], grads[10], grads[11], grads[12], grads[13], grads[14])
```

```python
import functools
import math

import jax
import jax.numpy as jnp
import ml_dtypes
import numpy as np
from jax import lax
from jax.experimental import pallas as pl
from jax.experimental.pallas import tpu as pltpu
from jax.sharding import PartitionSpec as P

LENGTH = 512


EPS = 1e-05


def plain_round(v):
    return lax.optimization_barrier(v.astype(jnp.bfloat16)).astype(jnp.float32)


def plain_same(v):
    return v


def value_keep(v):
    return (plain_round(v), None)


def value_pass(kept, grad):
    return (grad,)


def grad_keep(v):
    return (v, None)


def grad_round(kept, grad):
    return (plain_round(grad),)


def low(v):
    rounder = jax.custom_vjp(plain_round)
    rounder.defvjp(value_keep, value_pass)
    return rounder(v)


def low_back(v):
    rounder = jax.custom_vjp(plain_same)
    rounder.defvjp(grad_keep, grad_round)
    return rounder(v)


def matmul(first_factor, second_factor):
    return jnp.dot(first_factor, second_factor, preferred_element_type=jnp.float32)


def layer_norm(values, gain_row):
    centre = values - jnp.mean(values, axis=-1, keepdims=True)
    spread = jnp.mean(centre * centre, axis=-1, keepdims=True)
    return centre * lax.rsqrt(spread + EPS) * gain_row


MESH = pl.DeviceIdType.MESH
VMEM = pl.BlockSpec(memory_space=pltpu.VMEM)


def sinusoid_tables(length, model_width):
    offsets = (length - 1 - np.arange(2 * length - 1)).astype(np.float32)
    frequency = np.exp(
        np.arange(0, model_width, 2).astype(np.float32)
        * np.float32(-math.log(10000.0) / model_width)
    ).astype(np.float32)
    phases = offsets[:, None] * frequency[None, :]
    table = np.stack([np.sin(phases), np.cos(phases)], axis=-1).reshape(2 * length - 1, model_width)
    zero = np.zeros((1, model_width), np.float32)
    return (
        np.concatenate([table, zero]).astype(ml_dtypes.bfloat16),
        np.concatenate([table[::-1], zero]).astype(ml_dtypes.bfloat16),
    )


def tensor_kernel(factor, chunks, part, base, out, from_core, chip, from_row, send, recv):
    me = lax.axis_index("tensor")
    core = lax.rem(me, 2)
    sibling = me + 1 - 2 * core
    opposite = lax.rem(me + 2, 4)
    half = part.shape[0] // 2
    rows = half // chunks
    mine = core * half
    theirs = half - mine
    barrier = pltpu.get_barrier_semaphore()
    for other in (sibling, opposite):
        pl.semaphore_signal(barrier, inc=1, device_id={"tensor": other}, device_id_type=MESH)
    pl.semaphore_wait(barrier, 2)

    def span(start, c):
        return pl.ds(pl.multiple_of(start + c * rows, 8), rows)

    def remote(source, target, stage, c, device):
        return pltpu.make_async_remote_copy(
            src_ref=source,
            dst_ref=target,
            send_sem=send.at[stage, c],
            recv_sem=recv.at[stage, c],
            device_id={"tensor": device},
            device_id_type=MESH,
        )

    def first(c):
        return remote(part.at[span(theirs, c)], from_core.at[span(0, c)], 0, c, sibling)

    def second(c):
        return remote(chip.at[span(0, c)], from_row.at[span(0, c)], 1, c, opposite)

    def third(c):
        return remote(out.at[span(mine, c)], out.at[span(mine, c)], 2, c, sibling)

    for c in range(chunks):
        first(c).start()
    for c in range(chunks):
        first(c).wait_recv()
        chip[span(0, c), :] = part[span(mine, c), :] + from_core[span(0, c), :]
        second(c).start()
    for c in range(chunks):
        second(c).wait_recv()
        total = chip[span(0, c), :] + from_row[span(0, c), :]
        out[span(mine, c), :] = base[span(mine, c), :] + factor * total
        third(c).start()
    for c in range(chunks):
        first(c).wait_send()
        second(c).wait_send()
        third(c).wait_send()
        third(c).wait_recv()


def tensor_sum(base, part, factor, ident, chunks=8):
    rows, width = part.shape
    half = pltpu.VMEM((rows // 2, width), jnp.float32)
    return pl.pallas_call(
        functools.partial(tensor_kernel, factor, chunks),
        out_shape=jax.ShapeDtypeStruct((rows, width), jnp.float32),
        in_specs=[VMEM, VMEM],
        out_specs=VMEM,
        scratch_shapes=[
            half,
            half,
            half,
            pltpu.SemaphoreType.DMA((3, chunks)),
            pltpu.SemaphoreType.DMA((3, chunks)),
        ],
        compiler_params=pltpu.CompilerParams(
            collective_id=ident, has_side_effects=True, vmem_limit_bytes=16 * 2**20
        ),
        name="tensor_sum",
    )(part, base)


def exchange_kernel(axis, count, part, out, slots, send, recv):
    me = lax.axis_index(axis)
    barrier = pltpu.get_barrier_semaphore()

    def greet(step, carry):
        other = lax.rem(me + step, count)
        pl.semaphore_signal(barrier, inc=1, device_id={axis: other}, device_id_type=MESH)
        return carry

    lax.fori_loop(1, count, greet, 0)
    slots[me] = part[...]
    pl.semaphore_wait(barrier, count - 1)

    def copy(step):
        other = lax.rem(me + step, count)
        return pltpu.make_async_remote_copy(
            src_ref=part,
            dst_ref=slots.at[me],
            send_sem=send.at[step],
            recv_sem=recv.at[step],
            device_id={axis: other},
            device_id_type=MESH,
        )

    def begin(step, carry):
        copy(step).start()
        return carry

    def finish(step, carry):
        copy(step).wait_send()
        copy(step).wait_recv()
        return carry

    lax.fori_loop(1, count, begin, 0)
    lax.fori_loop(1, count, finish, 0)
    total = slots[0]
    for place in range(1, count):
        total = total + slots[place]
    out[...] = total


def exchange_sum(part, axis, ident):
    count = lax.axis_size(axis)
    return pl.pallas_call(
        functools.partial(exchange_kernel, axis, count),
        out_shape=jax.ShapeDtypeStruct(part.shape, jnp.float32),
        in_specs=[VMEM],
        out_specs=VMEM,
        scratch_shapes=[
            pltpu.VMEM((count,) + part.shape, jnp.float32),
            pltpu.SemaphoreType.DMA((count,)),
            pltpu.SemaphoreType.DMA((count,)),
        ],
        compiler_params=pltpu.CompilerParams(
            collective_id=ident, has_side_effects=True, vmem_limit_bytes=16 * 2**20
        ),
        name="exchange_" + axis,
    )(part)


def stack_rows(pieces, width):
    blocks = []
    starts = []
    filled = 0
    for piece in pieces:
        block = piece.reshape(-1, width)
        starts.append(filled)
        filled += block.shape[0]
        blocks.append(block)
    spare = -filled % 8
    if spare:
        blocks.append(jnp.zeros((spare, width), jnp.float32))
    return jnp.concatenate(blocks), starts


def exchange_many(pieces, axis, ident, width=128):
    packed, starts = stack_rows(pieces, width)
    summed = exchange_sum(packed, axis, ident)
    return [
        summed[start : start + piece.size // width].reshape(piece.shape)
        for piece, start in zip(pieces, starts)
    ]


def product(first_factor, second_factor, first_axis, second_axis):
    return lax.dot_general(
        first_factor,
        second_factor,
        (((first_axis,), (second_axis,)), ((), ())),
        preferred_element_type=jnp.float32,
    )


def head_mask(shape, head, head_size):
    lane = lax.broadcasted_iota(jnp.int32, shape, 1)
    return (lane >= head * head_size) & (lane < (head + 1) * head_size)


def attend_kernel(head_count, mixed, position, biases, out, weights, with_content, with_position):
    length = mixed.shape[0]
    width = out.shape[1]
    head_size = width // head_count
    queries = mixed[:, :width]
    keys = mixed[:, width : 2 * width].astype(jnp.bfloat16)
    values = mixed[:, 2 * width :].astype(jnp.bfloat16)
    with_content[...] = (queries + biases[0:1, :]).astype(jnp.bfloat16)
    with_position[...] = (queries + biases[1:2, :]).astype(jnp.bfloat16)
    attended = jnp.zeros((length, width), jnp.float32)
    for head in range(head_count):
        mask = head_mask((length, width), head, head_size)
        zero = jnp.zeros((length, width), jnp.bfloat16)
        content = product(jnp.where(mask, with_content[...], zero), keys, 1, 1)
        spread = product(jnp.where(mask, with_position[...], zero), position[...], 1, 1)
        relative = pltpu.roll(spread, length + 1, 1, stride=1, stride_axis=0)[:, :length]
        scores = (content + relative) * (1.0 / math.sqrt(head_size))
        top = jnp.max(scores, axis=1, keepdims=True)
        powers = jnp.exp(scores - top)
        share = (powers / jnp.sum(powers, axis=1, keepdims=True)).astype(jnp.bfloat16)
        weights[head] = share
        attended = jnp.where(mask, product(share, values, 1, 0), attended)
    out[...] = attended.astype(jnp.bfloat16)


def attend(mixed, position, biases, head_count):
    length = mixed.shape[0]
    width = mixed.shape[1] // 3
    flat = jax.ShapeDtypeStruct((length, width), jnp.bfloat16)
    return pl.pallas_call(
        functools.partial(attend_kernel, head_count),
        out_shape=(
            flat,
            jax.ShapeDtypeStruct((head_count, length, length), jnp.bfloat16),
            flat,
            flat,
        ),
        in_specs=[VMEM] * 3,
        out_specs=(VMEM,) * 4,
        compiler_params=pltpu.CompilerParams(vmem_limit_bytes=32 * 2**20),
        name="attend",
    )(mixed, position, biases)


def attend_back_kernel(
    head_count,
    grad_ref,
    mixed,
    reversed_position,
    weights,
    with_content,
    with_position,
    mixed_grad,
    position_grad,
    bias_grad,
):
    length, width = grad_ref.shape
    head_size = width // head_count
    row = lax.broadcasted_iota(jnp.int32, (length, length), 0)
    column = lax.broadcasted_iota(jnp.int32, (length, length), 1)
    flip = (row + column == length - 1).astype(jnp.float32).astype(jnp.bfloat16)
    zero = jnp.zeros((length, width), jnp.bfloat16)
    grad = grad_ref[...]
    keys = product(flip, mixed[:, width : 2 * width].astype(jnp.bfloat16), 1, 0).astype(jnp.bfloat16)
    values = product(flip, mixed[:, 2 * width :].astype(jnp.bfloat16), 1, 0).astype(jnp.bfloat16)
    value_grad = jnp.zeros((length, width), jnp.float32)
    key_grad = jnp.zeros((length, width), jnp.float32)
    content_grad = jnp.zeros((length, width), jnp.float32)
    spread_grad = jnp.zeros((length, width), jnp.float32)
    table_grad = jnp.zeros((2 * length, width), jnp.float32)
    for head in range(head_count):
        mask = head_mask((length, width), head, head_size)
        head_grad = jnp.where(mask, grad, zero)
        value_grad += product(weights[head], head_grad, 0, 0)
        share = product(weights[head], flip, 1, 0)
        share_grad = product(head_grad, values, 1, 1)
        inner = jnp.sum(share * share_grad, axis=1, keepdims=True)
        score_grad = (share * (share_grad - inner)).astype(jnp.bfloat16).astype(jnp.float32)
        score_grad = score_grad * (1.0 / math.sqrt(head_size))
        low_grad = score_grad.astype(jnp.bfloat16)
        content_grad = jnp.where(mask, product(low_grad, keys, 1, 0), content_grad)
        key_grad += product(low_grad, jnp.where(mask, with_content[...], zero), 0, 0)
        wide = jnp.concatenate([score_grad, jnp.zeros((length, length), jnp.float32)], axis=1)
        shifted = pltpu.roll(wide, 0, 1, stride=1, stride_axis=0).astype(jnp.bfloat16)
        spread_grad = jnp.where(mask, product(shifted, reversed_position[...], 1, 0), spread_grad)
        table_grad += product(shifted, jnp.where(mask, with_position[...], zero), 0, 0)
    mixed_grad[:, :width] = (content_grad + spread_grad).astype(jnp.bfloat16)
    mixed_grad[:, width : 2 * width] = product(flip, key_grad.astype(jnp.bfloat16), 1, 0).astype(
        jnp.bfloat16
    )
    mixed_grad[:, 2 * width :] = value_grad.astype(jnp.bfloat16)
    position_grad[...] = table_grad.astype(jnp.bfloat16)
    bias_grad[0:1, :] = jnp.sum(content_grad, axis=0, keepdims=True)
    bias_grad[1:2, :] = jnp.sum(spread_grad, axis=0, keepdims=True)


def attend_back(grad, mixed, reversed_position, kept, head_count):
    length, width = grad.shape
    return pl.pallas_call(
        functools.partial(attend_back_kernel, head_count),
        out_shape=(
            jax.ShapeDtypeStruct((length, 3 * width), jnp.bfloat16),
            jax.ShapeDtypeStruct((2 * length, width), jnp.bfloat16),
            jax.ShapeDtypeStruct((2, width), jnp.float32),
        ),
        in_specs=[VMEM] * 6,
        out_specs=(VMEM,) * 3,
        compiler_params=pltpu.CompilerParams(vmem_limit_bytes=32 * 2**20),
        name="attend_back",
    )(grad, mixed, reversed_position, *kept)


def sum_after(piece, earlier):
    if earlier is not None:
        piece, _ = lax.optimization_barrier((piece, earlier))
    return lax.psum(piece, "dp")


def attention_front(values, gain_row, weight):
    normed = low(layer_norm(values, gain_row))
    return low_back(matmul(normed, weight))


def attention_back(attended, weight_out):
    return low_back(matmul(attended, weight_out))


def feed_forward(values, gain_row, weight_in, weight_out):
    normed = low(layer_norm(values, gain_row))
    hidden = low_back(matmul(normed, weight_in))
    active = low(jax.nn.silu(hidden))
    return low_back(matmul(active, weight_out))


def depthwise_conv(gated, kernel):
    half = kernel.shape[0] // 2
    return lax.conv_general_dilated(
        gated,
        kernel[:, None, :],
        (1,),
        [(half, half)],
        dimension_numbers=("NWC", "WIO", "NWC"),
        feature_group_count=gated.shape[2],
        precision=lax.Precision.HIGHEST,
    )


def conv_front(values, gain_row, weight_in, kernel):
    channels = kernel.shape[1]
    normed = low(layer_norm(values, gain_row))
    paired = low_back(matmul(normed, weight_in.reshape(weight_in.shape[0], 2 * channels))).reshape(
        -1, 2, channels
    )
    gated = paired[:, 0] * jax.nn.sigmoid(paired[:, 1])
    return depthwise_conv(gated.reshape(-1, LENGTH, channels), kernel)


def conv_back(mixed_rows, batch_mean, batch_var, scale_row, shift_row, weight_out):
    scaled = (mixed_rows - batch_mean) * lax.rsqrt(batch_var + EPS) * scale_row + shift_row
    swished = low(jax.nn.silu(scaled)).reshape(-1, mixed_rows.shape[2])
    return low_back(matmul(swished, weight_out))


def per_device(
    inputs,
    norm_gains,
    early_up,
    early_down,
    query_key_value,
    position_weight,
    position_bias,
    attention_out,
    pointwise_in,
    depthwise,
    batch_gain,
    batch_bias,
    pointwise_out,
    late_up,
    late_down,
    output_cotangent,
):
    stream = inputs.astype(jnp.float32)
    gain_rows = norm_gains.astype(jnp.float32)
    early_in = early_up.astype(jnp.float32)
    early_back = early_down.astype(jnp.float32)
    project_qkv = query_key_value.astype(jnp.float32)
    query_bias = position_bias.astype(jnp.float32)
    project_out = attention_out.astype(jnp.float32)
    point_first = pointwise_in.astype(jnp.float32)
    depth_taps = depthwise.astype(jnp.float32)
    scale_row = batch_gain.astype(jnp.float32)
    shift_row = batch_bias.astype(jnp.float32)
    point_second = pointwise_out.astype(jnp.float32)
    late_in = late_up.astype(jnp.float32)
    late_back = late_down.astype(jnp.float32)
    first_part, first_pull = jax.vjp(feed_forward, stream, gain_rows[0], early_in, early_back)
    after_first = tensor_sum(stream, first_part, 0.5, 0)

    model_width, _, local_width = project_qkv.shape
    head_count = query_bias.shape[1]
    table, reversed_table = sinusoid_tables(LENGTH, model_width)
    low_pos = position_weight
    position = product(table, low_pos, 1, 0).astype(jnp.bfloat16)
    reversed_position = product(reversed_table, low_pos, 1, 0).astype(jnp.bfloat16)
    bias_rows = query_bias.reshape(2, local_width)
    mixed_qkv, qkv_pull = jax.vjp(
        attention_front,
        after_first,
        gain_rows[1],
        project_qkv.reshape(model_width, 3 * local_width),
    )
    attended, *kept = attend(mixed_qkv, position, bias_rows, head_count)
    second_part, out_pull = jax.vjp(attention_back, attended.astype(jnp.float32), project_out)
    after_second = tensor_sum(after_first, second_part, 1.0, 1)
    mixed_rows, front_pull = jax.vjp(
        conv_front, after_second, gain_rows[2], point_first, depth_taps
    )
    token_count = mixed_rows.shape[0] * mixed_rows.shape[1] * lax.axis_size("dp")
    sum_values, sum_squares = exchange_many(
        (jnp.sum(mixed_rows, axis=(0, 1)), jnp.sum(mixed_rows * mixed_rows, axis=(0, 1))), "dp", 8
    )
    batch_mean = sum_values / token_count
    batch_var = sum_squares / token_count - batch_mean * batch_mean
    third_part, back_pull = jax.vjp(
        conv_back, mixed_rows, batch_mean, batch_var, scale_row, shift_row, point_second
    )
    after_third = tensor_sum(after_second, third_part, 1.0, 2)
    fourth_part, fourth_pull = jax.vjp(feed_forward, after_third, gain_rows[3], late_in, late_back)
    after_fourth = tensor_sum(after_third, fourth_part, 0.5, 3)
    result, final_pull = jax.vjp(layer_norm, after_fourth, gain_rows[4])
    grad_four, gain_five = final_pull(output_cotangent.astype(jnp.float32))
    cotangent_in, gain_four, late_in_grad, late_back_grad = fourth_pull(0.5 * grad_four)
    late_sum = sum_after(jnp.concatenate([late_in_grad, late_back_grad]), None)
    grad_three = tensor_sum(grad_four, cotangent_in, 1.0, 4)
    direct_grad, mean_grad, var_grad, scale_grad, shift_grad, second_point_grad = back_pull(
        grad_three
    )
    mean_grad, var_grad = exchange_many((mean_grad, var_grad), "dp", 9)
    mixed_grad = (
        direct_grad + (mean_grad + 2.0 * var_grad * (mixed_rows - batch_mean)) / token_count
    )
    cotangent_in, gain_three, first_point_grad, depth_grad = front_pull(mixed_grad)
    second_point_grad = sum_after(second_point_grad, late_sum)
    first_point_grad = sum_after(
        first_point_grad.reshape(model_width, 2 * local_width), second_point_grad
    )
    grad_two = tensor_sum(grad_three, cotangent_in, 1.0, 5)
    attended_grad, out_grad = out_pull(grad_two)
    qkv_grad, position_grad, bias_grad = attend_back(
        attended_grad.astype(jnp.bfloat16), mixed_qkv, reversed_position, kept, head_count
    )
    pos_grad = product(reversed_table, position_grad, 0, 0)
    cotangent_in, gain_two, qkv_grad = qkv_pull(qkv_grad.astype(jnp.float32))
    out_grad = sum_after(out_grad, first_point_grad)
    middle_sum = sum_after(jnp.concatenate([qkv_grad, pos_grad], axis=1), out_grad)
    grad_one = tensor_sum(grad_two, cotangent_in, 1.0, 6)
    cotangent_in, gain_one, early_in_grad, early_back_grad = first_pull(0.5 * grad_one)
    early_sum = sum_after(jnp.concatenate([early_in_grad, early_back_grad]), middle_sum)
    grad_zero = tensor_sum(grad_one, cotangent_in, 1.0, 7)
    (gain_grads,) = exchange_many(
        (jnp.stack([gain_one, gain_two, gain_three, gain_four]),), "tensor", 10
    )
    gain_grads, gain_five, bias_grad, depth_grad, scale_grad, shift_grad = exchange_many(
        (gain_grads, gain_five, bias_grad, depth_grad, scale_grad, shift_grad), "dp", 11
    )
    return (
        result.astype(jnp.bfloat16),
        grad_zero,
        jnp.concatenate([gain_grads, gain_five[None]]),
        early_sum[:model_width],
        early_sum[model_width:],
        middle_sum[:, : 3 * local_width].reshape(query_key_value.shape),
        middle_sum[:, 3 * local_width :],
        bias_grad.reshape(position_bias.shape),
        out_grad,
        first_point_grad.reshape(pointwise_in.shape),
        depth_grad,
        scale_grad,
        shift_grad,
        second_point_grad,
        late_sum[:model_width],
        late_sum[model_width:],
    )


def solution(mesh):
    return jax.shard_map(
        per_device,
        mesh=mesh,
        in_specs=(
            P("dp", None),
            P(),
            P(None, "tensor"),
            P("tensor", None),
            P(None, None, "tensor"),
            P(None, "tensor"),
            P(None, "tensor", None),
            P("tensor", None),
            P(None, None, "tensor"),
            P(None, "tensor"),
            P("tensor"),
            P("tensor"),
            P("tensor", None),
            P(None, "tensor"),
            P("tensor", None),
            P("dp", None),
        ),
        out_specs=(
            P("dp", None),
            P("dp", None),
            P(),
            P(None, "tensor"),
            P("tensor", None),
            P(None, None, "tensor"),
            P(None, "tensor"),
            P(None, "tensor", None),
            P("tensor", None),
            P(None, None, "tensor"),
            P(None, "tensor"),
            P("tensor"),
            P("tensor"),
            P("tensor", None),
            P(None, "tensor"),
            P("tensor", None),
        ),
        check_vma=False,
    )
```

```python
import functools
import math

import jax
import jax.numpy as jnp
import ml_dtypes
import numpy as np
from jax import lax
from jax.experimental import pallas as pl
from jax.experimental.pallas import tpu as pltpu
from jax.sharding import PartitionSpec as P

LENGTH = 512


EPS = 1e-05


def plain_round(v):
    return lax.optimization_barrier(v.astype(jnp.bfloat16)).astype(jnp.float32)


def plain_same(v):
    return v


def value_keep(v):
    return (plain_round(v), None)


def value_pass(kept, grad):
    return (grad,)


def grad_keep(v):
    return (v, None)


def grad_round(kept, grad):
    return (plain_round(grad),)


def low(v):
    rounder = jax.custom_vjp(plain_round)
    rounder.defvjp(value_keep, value_pass)
    return rounder(v)


def low_back(v):
    rounder = jax.custom_vjp(plain_same)
    rounder.defvjp(grad_keep, grad_round)
    return rounder(v)


def matmul(first_factor, second_factor):
    return jnp.dot(first_factor, second_factor, preferred_element_type=jnp.float32)


def layer_norm(values, gain_row):
    centre = values - jnp.mean(values, axis=-1, keepdims=True)
    spread = jnp.mean(centre * centre, axis=-1, keepdims=True)
    return centre * lax.rsqrt(spread + EPS) * gain_row


MESH = pl.DeviceIdType.MESH
VMEM = pl.BlockSpec(memory_space=pltpu.VMEM)


def sinusoid_tables(length, model_width):
    offsets = (length - 1 - np.arange(2 * length - 1)).astype(np.float32)
    frequency = np.exp(
        np.arange(0, model_width, 2).astype(np.float32)
        * np.float32(-math.log(10000.0) / model_width)
    ).astype(np.float32)
    phases = offsets[:, None] * frequency[None, :]
    table = np.stack([np.sin(phases), np.cos(phases)], axis=-1).reshape(2 * length - 1, model_width)
    zero = np.zeros((1, model_width), np.float32)
    return (
        np.concatenate([table, zero]).astype(ml_dtypes.bfloat16),
        np.concatenate([table[::-1], zero]).astype(ml_dtypes.bfloat16),
    )


def tensor_kernel(factor, chunks, part, base, out, from_core, chip, from_row, send, recv):
    me = lax.axis_index("tensor")
    core = lax.rem(me, 2)
    sibling = me + 1 - 2 * core
    opposite = lax.rem(me + 2, 4)
    half = part.shape[0] // 2
    rows = half // chunks
    mine = core * half
    theirs = half - mine
    barrier = pltpu.get_barrier_semaphore()
    for other in (sibling, opposite):
        pl.semaphore_signal(barrier, inc=1, device_id={"tensor": other}, device_id_type=MESH)
    pl.semaphore_wait(barrier, 2)

    def span(start, c):
        return pl.ds(pl.multiple_of(start + c * rows, 8), rows)

    def remote(source, target, stage, c, device):
        return pltpu.make_async_remote_copy(
            src_ref=source,
            dst_ref=target,
            send_sem=send.at[stage, c],
            recv_sem=recv.at[stage, c],
            device_id={"tensor": device},
            device_id_type=MESH,
        )

    def first(c):
        return remote(part.at[span(theirs, c)], from_core.at[span(0, c)], 0, c, sibling)

    def second(c):
        return remote(chip.at[span(0, c)], from_row.at[span(0, c)], 1, c, opposite)

    def third(c):
        return remote(out.at[span(mine, c)], out.at[span(mine, c)], 2, c, sibling)

    for c in range(chunks):
        first(c).start()
    for c in range(chunks):
        first(c).wait_recv()
        chip[span(0, c), :] = part[span(mine, c), :] + from_core[span(0, c), :]
        second(c).start()
    for c in range(chunks):
        second(c).wait_recv()
        total = chip[span(0, c), :] + from_row[span(0, c), :]
        out[span(mine, c), :] = base[span(mine, c), :] + factor * total
        third(c).start()
    for c in range(chunks):
        first(c).wait_send()
        second(c).wait_send()
        third(c).wait_send()
        third(c).wait_recv()


def tensor_sum(base, part, factor, ident, chunks=8):
    rows, width = part.shape
    half = pltpu.VMEM((rows // 2, width), jnp.float32)
    return pl.pallas_call(
        functools.partial(tensor_kernel, factor, chunks),
        out_shape=jax.ShapeDtypeStruct((rows, width), jnp.float32),
        in_specs=[VMEM, VMEM],
        out_specs=VMEM,
        scratch_shapes=[
            half,
            half,
            half,
            pltpu.SemaphoreType.DMA((3, chunks)),
            pltpu.SemaphoreType.DMA((3, chunks)),
        ],
        compiler_params=pltpu.CompilerParams(
            collective_id=ident, has_side_effects=True, vmem_limit_bytes=16 * 2**20
        ),
        name="tensor_sum",
    )(part, base)


def exchange_kernel(axis, count, part, out, slots, send, recv):
    me = lax.axis_index(axis)
    barrier = pltpu.get_barrier_semaphore()

    def greet(step, carry):
        other = lax.rem(me + step, count)
        pl.semaphore_signal(barrier, inc=1, device_id={axis: other}, device_id_type=MESH)
        return carry

    lax.fori_loop(1, count, greet, 0)
    slots[me] = part[...]
    pl.semaphore_wait(barrier, count - 1)

    def copy(step):
        other = lax.rem(me + step, count)
        return pltpu.make_async_remote_copy(
            src_ref=part,
            dst_ref=slots.at[me],
            send_sem=send.at[step],
            recv_sem=recv.at[step],
            device_id={axis: other},
            device_id_type=MESH,
        )

    def begin(step, carry):
        copy(step).start()
        return carry

    def finish(step, carry):
        copy(step).wait_send()
        copy(step).wait_recv()
        return carry

    lax.fori_loop(1, count, begin, 0)
    lax.fori_loop(1, count, finish, 0)
    total = slots[0]
    for place in range(1, count):
        total = total + slots[place]
    out[...] = total


def exchange_sum(part, axis, ident):
    count = lax.axis_size(axis)
    return pl.pallas_call(
        functools.partial(exchange_kernel, axis, count),
        out_shape=jax.ShapeDtypeStruct(part.shape, jnp.float32),
        in_specs=[VMEM],
        out_specs=VMEM,
        scratch_shapes=[
            pltpu.VMEM((count,) + part.shape, jnp.float32),
            pltpu.SemaphoreType.DMA((count,)),
            pltpu.SemaphoreType.DMA((count,)),
        ],
        compiler_params=pltpu.CompilerParams(
            collective_id=ident, has_side_effects=True, vmem_limit_bytes=16 * 2**20
        ),
        name="exchange_" + axis,
    )(part)


def stack_rows(pieces, width):
    blocks = []
    starts = []
    filled = 0
    for piece in pieces:
        block = piece.reshape(-1, width)
        starts.append(filled)
        filled += block.shape[0]
        blocks.append(block)
    spare = -filled % 8
    if spare:
        blocks.append(jnp.zeros((spare, width), jnp.float32))
    return jnp.concatenate(blocks), starts


def exchange_many(pieces, axis, ident, width=128):
    packed, starts = stack_rows(pieces, width)
    summed = exchange_sum(packed, axis, ident)
    return [
        summed[start : start + piece.size // width].reshape(piece.shape)
        for piece, start in zip(pieces, starts)
    ]


def product(first_factor, second_factor, first_axis, second_axis):
    return lax.dot_general(
        first_factor,
        second_factor,
        (((first_axis,), (second_axis,)), ((), ())),
        preferred_element_type=jnp.float32,
    )


def head_mask(shape, head, head_size):
    lane = lax.broadcasted_iota(jnp.int32, shape, 1)
    return (lane >= head * head_size) & (lane < (head + 1) * head_size)


def attend_kernel(head_count, mixed, position, biases, out, weights, with_content, with_position):
    length = mixed.shape[0]
    width = out.shape[1]
    head_size = width // head_count
    queries = mixed[:, :width]
    keys = mixed[:, width : 2 * width].astype(jnp.bfloat16)
    values = mixed[:, 2 * width :].astype(jnp.bfloat16)
    with_content[...] = (queries + biases[0:1, :]).astype(jnp.bfloat16)
    with_position[...] = (queries + biases[1:2, :]).astype(jnp.bfloat16)
    attended = jnp.zeros((length, width), jnp.float32)
    for head in range(head_count):
        mask = head_mask((length, width), head, head_size)
        zero = jnp.zeros((length, width), jnp.bfloat16)
        content = product(jnp.where(mask, with_content[...], zero), keys, 1, 1)
        spread = product(jnp.where(mask, with_position[...], zero), position[...], 1, 1)
        relative = pltpu.roll(spread, length + 1, 1, stride=1, stride_axis=0)[:, :length]
        scores = (content + relative) * (1.0 / math.sqrt(head_size))
        top = jnp.max(scores, axis=1, keepdims=True)
        powers = jnp.exp(scores - top)
        share = (powers / jnp.sum(powers, axis=1, keepdims=True)).astype(jnp.bfloat16)
        weights[head] = share
        attended = jnp.where(mask, product(share, values, 1, 0), attended)
    out[...] = attended.astype(jnp.bfloat16)


def attend(mixed, position, biases, head_count):
    length = mixed.shape[0]
    width = mixed.shape[1] // 3
    flat = jax.ShapeDtypeStruct((length, width), jnp.bfloat16)
    return pl.pallas_call(
        functools.partial(attend_kernel, head_count),
        out_shape=(
            flat,
            jax.ShapeDtypeStruct((head_count, length, length), jnp.bfloat16),
            flat,
            flat,
        ),
        in_specs=[VMEM] * 3,
        out_specs=(VMEM,) * 4,
        compiler_params=pltpu.CompilerParams(vmem_limit_bytes=32 * 2**20),
        name="attend",
    )(mixed, position, biases)


def attend_back_kernel(
    head_count,
    grad_ref,
    mixed,
    reversed_position,
    weights,
    with_content,
    with_position,
    mixed_grad,
    position_grad,
    bias_grad,
):
    length, width = grad_ref.shape
    head_size = width // head_count
    row = lax.broadcasted_iota(jnp.int32, (length, length), 0)
    column = lax.broadcasted_iota(jnp.int32, (length, length), 1)
    flip = (row + column == length - 1).astype(jnp.float32).astype(jnp.bfloat16)
    zero = jnp.zeros((length, width), jnp.bfloat16)
    grad = grad_ref[...]
    keys = product(flip, mixed[:, width : 2 * width].astype(jnp.bfloat16), 1, 0).astype(jnp.bfloat16)
    values = product(flip, mixed[:, 2 * width :].astype(jnp.bfloat16), 1, 0).astype(jnp.bfloat16)
    value_grad = jnp.zeros((length, width), jnp.float32)
    key_grad = jnp.zeros((length, width), jnp.float32)
    content_grad = jnp.zeros((length, width), jnp.float32)
    spread_grad = jnp.zeros((length, width), jnp.float32)
    table_grad = jnp.zeros((2 * length, width), jnp.float32)
    for head in range(head_count):
        mask = head_mask((length, width), head, head_size)
        head_grad = jnp.where(mask, grad, zero)
        value_grad += product(weights[head], head_grad, 0, 0)
        share = product(weights[head], flip, 1, 0)
        share_grad = product(head_grad, values, 1, 1)
        inner = jnp.sum(share * share_grad, axis=1, keepdims=True)
        score_grad = (share * (share_grad - inner)).astype(jnp.bfloat16).astype(jnp.float32)
        score_grad = score_grad * (1.0 / math.sqrt(head_size))
        low_grad = score_grad.astype(jnp.bfloat16)
        content_grad = jnp.where(mask, product(low_grad, keys, 1, 0), content_grad)
        key_grad += product(low_grad, jnp.where(mask, with_content[...], zero), 0, 0)
        wide = jnp.concatenate([score_grad, jnp.zeros((length, length), jnp.float32)], axis=1)
        shifted = pltpu.roll(wide, 0, 1, stride=1, stride_axis=0).astype(jnp.bfloat16)
        spread_grad = jnp.where(mask, product(shifted, reversed_position[...], 1, 0), spread_grad)
        table_grad += product(shifted, jnp.where(mask, with_position[...], zero), 0, 0)
    mixed_grad[:, :width] = (content_grad + spread_grad).astype(jnp.bfloat16)
    mixed_grad[:, width : 2 * width] = product(flip, key_grad.astype(jnp.bfloat16), 1, 0).astype(
        jnp.bfloat16
    )
    mixed_grad[:, 2 * width :] = value_grad.astype(jnp.bfloat16)
    position_grad[...] = table_grad.astype(jnp.bfloat16)
    bias_grad[0:1, :] = jnp.sum(content_grad, axis=0, keepdims=True)
    bias_grad[1:2, :] = jnp.sum(spread_grad, axis=0, keepdims=True)


def attend_back(grad, mixed, reversed_position, kept, head_count):
    length, width = grad.shape
    return pl.pallas_call(
        functools.partial(attend_back_kernel, head_count),
        out_shape=(
            jax.ShapeDtypeStruct((length, 3 * width), jnp.bfloat16),
            jax.ShapeDtypeStruct((2 * length, width), jnp.bfloat16),
            jax.ShapeDtypeStruct((2, width), jnp.float32),
        ),
        in_specs=[VMEM] * 6,
        out_specs=(VMEM,) * 3,
        compiler_params=pltpu.CompilerParams(vmem_limit_bytes=32 * 2**20),
        name="attend_back",
    )(grad, mixed, reversed_position, *kept)


def halving_kernel(count, groups, part, out, work, land, send, recv):
    me = lax.axis_index("dp")
    bits = [1 << k for k in range(count.bit_length() - 1)]
    orders = [bits, bits[1:] + bits[:1]]
    stages = len(bits)
    height = part.shape[0] // groups
    barrier = pltpu.get_barrier_semaphore()

    def side(bit):
        return lax.rem(me // bit, 2)

    def partner(bit):
        return me + bit * (1 - 2 * side(bit))

    for bit in bits:
        pl.semaphore_signal(barrier, inc=1, device_id={"dp": partner(bit)}, device_id_type=MESH)
    pl.semaphore_wait(barrier, stages)

    def span(start, size):
        return pl.ds(pl.multiple_of(start, 8), size)

    spans = []
    for group in range(groups):
        start = group * height
        steps = []
        for k, bit in enumerate(orders[group % 2]):
            size = height >> (k + 1)
            keep = start + side(bit) * size
            give = start + (1 - side(bit)) * size
            steps.append((bit, span(keep, size), span(give, size)))
            start = keep
        spans.append(steps)

    def landing(group, k):
        return pl.ds(group * height + height - (height >> k), height >> (k + 1))

    def remote(source, target, group, stage, bit):
        return pltpu.make_async_remote_copy(
            src_ref=source,
            dst_ref=target,
            send_sem=send.at[group, stage],
            recv_sem=recv.at[group, stage],
            device_id={"dp": partner(bit)},
            device_id_type=MESH,
        )

    def down(group, k):
        bit, _, give = spans[group][k]
        source = part if k == 0 else work
        return remote(source.at[give], land.at[landing(group, k)], group, k, bit)

    def up(group, k):
        bit, keep, _ = spans[group][k]
        return remote(out.at[keep], out.at[keep], group, stages + k, bit)

    for group in range(groups):
        down(group, 0).start()
    for k in range(stages):
        for group in range(groups):
            keep = spans[group][k][1]
            source = part if k == 0 else work
            down(group, k).wait_recv()
            total = source[keep, :] + land[landing(group, k), :]
            if k < stages - 1:
                work[keep, :] = total
                down(group, k + 1).start()
            else:
                out[keep, :] = total
                up(group, k).start()
    for k in reversed(range(stages)):
        for group in range(groups):
            up(group, k).wait_recv()
            if k > 0:
                up(group, k - 1).start()
    for group in range(groups):
        for k in range(stages):
            down(group, k).wait_send()
            up(group, k).wait_send()


def halving_sum(part, ident, groups=4):
    count = lax.axis_size("dp")
    stages = count.bit_length() - 1
    buffer = pltpu.VMEM(part.shape, jnp.float32)
    return pl.pallas_call(
        functools.partial(halving_kernel, count, groups),
        out_shape=jax.ShapeDtypeStruct(part.shape, jnp.float32),
        in_specs=[VMEM],
        out_specs=VMEM,
        scratch_shapes=[
            buffer,
            buffer,
            pltpu.SemaphoreType.DMA((groups, 2 * stages)),
            pltpu.SemaphoreType.DMA((groups, 2 * stages)),
        ],
        compiler_params=pltpu.CompilerParams(
            collective_id=ident, has_side_effects=True, vmem_limit_bytes=32 * 2**20
        ),
        name="halving_sum",
    )(part)


def attention_front(values, gain_row, weight):
    normed = low(layer_norm(values, gain_row))
    return low_back(matmul(normed, weight))


def attention_back(attended, weight_out):
    return low_back(matmul(attended, weight_out))


def feed_forward(values, gain_row, weight_in, weight_out):
    normed = low(layer_norm(values, gain_row))
    hidden = low_back(matmul(normed, weight_in))
    active = low(jax.nn.silu(hidden))
    return low_back(matmul(active, weight_out))


def depthwise_conv(gated, kernel):
    half = kernel.shape[0] // 2
    return lax.conv_general_dilated(
        gated,
        kernel[:, None, :],
        (1,),
        [(half, half)],
        dimension_numbers=("NWC", "WIO", "NWC"),
        feature_group_count=gated.shape[2],
        precision=lax.Precision.HIGHEST,
    )


def conv_front(values, gain_row, weight_in, kernel):
    channels = kernel.shape[1]
    normed = low(layer_norm(values, gain_row))
    paired = low_back(matmul(normed, weight_in.reshape(weight_in.shape[0], 2 * channels))).reshape(
        -1, 2, channels
    )
    gated = paired[:, 0] * jax.nn.sigmoid(paired[:, 1])
    return depthwise_conv(gated.reshape(-1, LENGTH, channels), kernel)


def conv_back(mixed_rows, batch_mean, batch_var, scale_row, shift_row, weight_out):
    scaled = (mixed_rows - batch_mean) * lax.rsqrt(batch_var + EPS) * scale_row + shift_row
    swished = low(jax.nn.silu(scaled)).reshape(-1, mixed_rows.shape[2])
    return low_back(matmul(swished, weight_out))


def per_device(
    inputs,
    norm_gains,
    early_up,
    early_down,
    query_key_value,
    position_weight,
    position_bias,
    attention_out,
    pointwise_in,
    depthwise,
    batch_gain,
    batch_bias,
    pointwise_out,
    late_up,
    late_down,
    output_cotangent,
):
    stream = inputs.astype(jnp.float32)
    gain_rows = norm_gains.astype(jnp.float32)
    early_in = early_up.astype(jnp.float32)
    early_back = early_down.astype(jnp.float32)
    project_qkv = query_key_value.astype(jnp.float32)
    query_bias = position_bias.astype(jnp.float32)
    project_out = attention_out.astype(jnp.float32)
    point_first = pointwise_in.astype(jnp.float32)
    depth_taps = depthwise.astype(jnp.float32)
    scale_row = batch_gain.astype(jnp.float32)
    shift_row = batch_bias.astype(jnp.float32)
    point_second = pointwise_out.astype(jnp.float32)
    late_in = late_up.astype(jnp.float32)
    late_back = late_down.astype(jnp.float32)
    first_part, first_pull = jax.vjp(feed_forward, stream, gain_rows[0], early_in, early_back)
    after_first = tensor_sum(stream, first_part, 0.5, 0)

    model_width, _, local_width = project_qkv.shape
    head_count = query_bias.shape[1]
    table, reversed_table = sinusoid_tables(LENGTH, model_width)
    low_pos = position_weight
    position = product(table, low_pos, 1, 0).astype(jnp.bfloat16)
    reversed_position = product(reversed_table, low_pos, 1, 0).astype(jnp.bfloat16)
    bias_rows = query_bias.reshape(2, local_width)
    mixed_qkv, qkv_pull = jax.vjp(
        attention_front,
        after_first,
        gain_rows[1],
        project_qkv.reshape(model_width, 3 * local_width),
    )
    attended, *kept = attend(mixed_qkv, position, bias_rows, head_count)
    second_part, out_pull = jax.vjp(attention_back, attended.astype(jnp.float32), project_out)
    after_second = tensor_sum(after_first, second_part, 1.0, 1)
    mixed_rows, front_pull = jax.vjp(
        conv_front, after_second, gain_rows[2], point_first, depth_taps
    )
    token_count = mixed_rows.shape[0] * mixed_rows.shape[1] * lax.axis_size("dp")
    sum_values, sum_squares = exchange_many(
        (jnp.sum(mixed_rows, axis=(0, 1)), jnp.sum(mixed_rows * mixed_rows, axis=(0, 1))), "dp", 8
    )
    batch_mean = sum_values / token_count
    batch_var = sum_squares / token_count - batch_mean * batch_mean
    third_part, back_pull = jax.vjp(
        conv_back, mixed_rows, batch_mean, batch_var, scale_row, shift_row, point_second
    )
    after_third = tensor_sum(after_second, third_part, 1.0, 2)
    fourth_part, fourth_pull = jax.vjp(feed_forward, after_third, gain_rows[3], late_in, late_back)
    after_fourth = tensor_sum(after_third, fourth_part, 0.5, 3)
    result, final_pull = jax.vjp(layer_norm, after_fourth, gain_rows[4])
    grad_four, gain_five = final_pull(output_cotangent.astype(jnp.float32))
    cotangent_in, gain_four, late_in_grad, late_back_grad = fourth_pull(0.5 * grad_four)
    late_in_grad, late_back_grad = lax.psum((late_in_grad, late_back_grad), "dp")
    grad_three = tensor_sum(grad_four, cotangent_in, 1.0, 4)
    direct_grad, mean_grad, var_grad, scale_grad, shift_grad, second_point_grad = back_pull(
        grad_three
    )
    mean_grad, var_grad = exchange_many((mean_grad, var_grad), "dp", 9)
    mixed_grad = (
        direct_grad + (mean_grad + 2.0 * var_grad * (mixed_rows - batch_mean)) / token_count
    )
    cotangent_in, gain_three, first_point_grad, depth_grad = front_pull(mixed_grad)
    grad_two = tensor_sum(grad_three, cotangent_in, 1.0, 5)
    attended_grad, out_grad = out_pull(grad_two)
    qkv_grad, position_grad, bias_grad = attend_back(
        attended_grad.astype(jnp.bfloat16), mixed_qkv, reversed_position, kept, head_count
    )
    pos_grad = product(reversed_table, position_grad, 0, 0)
    cotangent_in, gain_two, qkv_grad = qkv_pull(qkv_grad.astype(jnp.float32))
    grad_one = tensor_sum(grad_two, cotangent_in, 1.0, 6)
    cotangent_in, gain_one, early_in_grad, early_back_grad = first_pull(0.5 * grad_one)
    first_point_grad = first_point_grad.reshape(model_width, 2 * local_width)
    fold = model_width // 2
    pieces = (
        early_in_grad,
        early_back_grad,
        jnp.concatenate([qkv_grad, pos_grad], axis=1),
        jnp.concatenate([first_point_grad[:fold], first_point_grad[fold:]], axis=1),
        out_grad,
        second_point_grad,
    )
    summed = halving_sum(jnp.concatenate(pieces), 12)
    early_in_grad, early_back_grad, middle_sum, first_sum, out_grad, second_point_grad = jnp.split(
        summed, np.cumsum([piece.shape[0] for piece in pieces])[:-1].tolist()
    )
    first_point_grad = jnp.concatenate(
        [first_sum[:, : 2 * local_width], first_sum[:, 2 * local_width :]]
    )
    grad_zero = tensor_sum(grad_one, cotangent_in, 1.0, 7)
    (gain_grads,) = exchange_many(
        (jnp.stack([gain_one, gain_two, gain_three, gain_four]),), "tensor", 10
    )
    gain_grads, gain_five, bias_grad, depth_grad, scale_grad, shift_grad = exchange_many(
        (gain_grads, gain_five, bias_grad, depth_grad, scale_grad, shift_grad), "dp", 11
    )
    return (
        result.astype(jnp.bfloat16),
        grad_zero,
        jnp.concatenate([gain_grads, gain_five[None]]),
        early_in_grad,
        early_back_grad,
        middle_sum[:, : 3 * local_width].reshape(query_key_value.shape),
        middle_sum[:, 3 * local_width :],
        bias_grad.reshape(position_bias.shape),
        out_grad,
        first_point_grad.reshape(pointwise_in.shape),
        depth_grad,
        scale_grad,
        shift_grad,
        second_point_grad,
        late_in_grad,
        late_back_grad,
    )


def solution(mesh):
    return jax.shard_map(
        per_device,
        mesh=mesh,
        in_specs=(
            P("dp", None),
            P(),
            P(None, "tensor"),
            P("tensor", None),
            P(None, None, "tensor"),
            P(None, "tensor"),
            P(None, "tensor", None),
            P("tensor", None),
            P(None, None, "tensor"),
            P(None, "tensor"),
            P("tensor"),
            P("tensor"),
            P("tensor", None),
            P(None, "tensor"),
            P("tensor", None),
            P("dp", None),
        ),
        out_specs=(
            P("dp", None),
            P("dp", None),
            P(),
            P(None, "tensor"),
            P("tensor", None),
            P(None, None, "tensor"),
            P(None, "tensor"),
            P(None, "tensor", None),
            P("tensor", None),
            P(None, None, "tensor"),
            P(None, "tensor"),
            P("tensor"),
            P("tensor"),
            P("tensor", None),
            P(None, "tensor"),
            P("tensor", None),
        ),
        check_vma=False,
    )
```

```python
import functools
import math

import jax
import jax.numpy as jnp
import ml_dtypes
import numpy as np
from jax import lax
from jax.experimental import pallas as pl
from jax.experimental.pallas import tpu as pltpu
from jax.sharding import PartitionSpec as P

LENGTH = 512


EPS = 1e-05


def plain_round(v):
    return lax.optimization_barrier(v.astype(jnp.bfloat16)).astype(jnp.float32)


def plain_same(v):
    return v


def value_keep(v):
    return (plain_round(v), None)


def value_pass(kept, grad):
    return (grad,)


def grad_keep(v):
    return (v, None)


def grad_round(kept, grad):
    return (plain_round(grad),)


def low(v):
    rounder = jax.custom_vjp(plain_round)
    rounder.defvjp(value_keep, value_pass)
    return rounder(v)


def low_back(v):
    rounder = jax.custom_vjp(plain_same)
    rounder.defvjp(grad_keep, grad_round)
    return rounder(v)


def matmul(first_factor, second_factor):
    return jnp.dot(first_factor, second_factor, preferred_element_type=jnp.float32)


def layer_norm(values, gain_row):
    centre = values - jnp.mean(values, axis=-1, keepdims=True)
    spread = jnp.mean(centre * centre, axis=-1, keepdims=True)
    return centre * lax.rsqrt(spread + EPS) * gain_row


MESH = pl.DeviceIdType.MESH
VMEM = pl.BlockSpec(memory_space=pltpu.VMEM)


def sinusoid_tables(length, model_width):
    offsets = (length - 1 - np.arange(2 * length - 1)).astype(np.float32)
    frequency = np.exp(
        np.arange(0, model_width, 2).astype(np.float32)
        * np.float32(-math.log(10000.0) / model_width)
    ).astype(np.float32)
    phases = offsets[:, None] * frequency[None, :]
    table = np.stack([np.sin(phases), np.cos(phases)], axis=-1).reshape(2 * length - 1, model_width)
    zero = np.zeros((1, model_width), np.float32)
    return (
        np.concatenate([table, zero]).astype(ml_dtypes.bfloat16),
        np.concatenate([table[::-1], zero]).astype(ml_dtypes.bfloat16),
    )


def tensor_kernel(factor, chunks, part, base, out, from_core, chip, from_row, send, recv):
    me = lax.axis_index("tensor")
    core = lax.rem(me, 2)
    sibling = me + 1 - 2 * core
    opposite = lax.rem(me + 2, 4)
    half = part.shape[0] // 2
    rows = half // chunks
    mine = core * half
    theirs = half - mine
    barrier = pltpu.get_barrier_semaphore()
    for other in (sibling, opposite):
        pl.semaphore_signal(barrier, inc=1, device_id={"tensor": other}, device_id_type=MESH)
    pl.semaphore_wait(barrier, 2)

    def span(start, c):
        return pl.ds(pl.multiple_of(start + c * rows, 8), rows)

    def remote(source, target, stage, c, device):
        return pltpu.make_async_remote_copy(
            src_ref=source,
            dst_ref=target,
            send_sem=send.at[stage, c],
            recv_sem=recv.at[stage, c],
            device_id={"tensor": device},
            device_id_type=MESH,
        )

    def first(c):
        return remote(part.at[span(theirs, c)], from_core.at[span(0, c)], 0, c, sibling)

    def second(c):
        return remote(chip.at[span(0, c)], from_row.at[span(0, c)], 1, c, opposite)

    def third(c):
        return remote(out.at[span(mine, c)], out.at[span(mine, c)], 2, c, sibling)

    for c in range(chunks):
        first(c).start()
    for c in range(chunks):
        first(c).wait_recv()
        chip[span(0, c), :] = part[span(mine, c), :] + from_core[span(0, c), :]
        second(c).start()
    for c in range(chunks):
        second(c).wait_recv()
        total = chip[span(0, c), :] + from_row[span(0, c), :]
        out[span(mine, c), :] = base[span(mine, c), :] + factor * total
        third(c).start()
    for c in range(chunks):
        first(c).wait_send()
        second(c).wait_send()
        third(c).wait_send()
        third(c).wait_recv()


def tensor_sum(base, part, factor, ident, chunks=8):
    rows, width = part.shape
    half = pltpu.VMEM((rows // 2, width), jnp.float32)
    return pl.pallas_call(
        functools.partial(tensor_kernel, factor, chunks),
        out_shape=jax.ShapeDtypeStruct((rows, width), jnp.float32),
        in_specs=[VMEM, VMEM],
        out_specs=VMEM,
        scratch_shapes=[
            half,
            half,
            half,
            pltpu.SemaphoreType.DMA((3, chunks)),
            pltpu.SemaphoreType.DMA((3, chunks)),
        ],
        compiler_params=pltpu.CompilerParams(
            collective_id=ident, has_side_effects=True, vmem_limit_bytes=16 * 2**20
        ),
        name="tensor_sum",
    )(part, base)


def exchange_kernel(axis, count, part, out, slots, send, recv):
    me = lax.axis_index(axis)
    barrier = pltpu.get_barrier_semaphore()

    def greet(step, carry):
        other = lax.rem(me + step, count)
        pl.semaphore_signal(barrier, inc=1, device_id={axis: other}, device_id_type=MESH)
        return carry

    lax.fori_loop(1, count, greet, 0)
    slots[me] = part[...]
    pl.semaphore_wait(barrier, count - 1)

    def copy(step):
        other = lax.rem(me + step, count)
        return pltpu.make_async_remote_copy(
            src_ref=part,
            dst_ref=slots.at[me],
            send_sem=send.at[step],
            recv_sem=recv.at[step],
            device_id={axis: other},
            device_id_type=MESH,
        )

    def begin(step, carry):
        copy(step).start()
        return carry

    def finish(step, carry):
        copy(step).wait_send()
        copy(step).wait_recv()
        return carry

    lax.fori_loop(1, count, begin, 0)
    lax.fori_loop(1, count, finish, 0)
    total = slots[0]
    for place in range(1, count):
        total = total + slots[place]
    out[...] = total


def exchange_sum(part, axis, ident):
    count = lax.axis_size(axis)
    return pl.pallas_call(
        functools.partial(exchange_kernel, axis, count),
        out_shape=jax.ShapeDtypeStruct(part.shape, jnp.float32),
        in_specs=[VMEM],
        out_specs=VMEM,
        scratch_shapes=[
            pltpu.VMEM((count,) + part.shape, jnp.float32),
            pltpu.SemaphoreType.DMA((count,)),
            pltpu.SemaphoreType.DMA((count,)),
        ],
        compiler_params=pltpu.CompilerParams(
            collective_id=ident, has_side_effects=True, vmem_limit_bytes=16 * 2**20
        ),
        name="exchange_" + axis,
    )(part)


def stack_rows(pieces, width):
    blocks = []
    starts = []
    filled = 0
    for piece in pieces:
        block = piece.reshape(-1, width)
        starts.append(filled)
        filled += block.shape[0]
        blocks.append(block)
    spare = -filled % 8
    if spare:
        blocks.append(jnp.zeros((spare, width), jnp.float32))
    return jnp.concatenate(blocks), starts


def exchange_many(pieces, axis, ident, width=128):
    packed, starts = stack_rows(pieces, width)
    summed = exchange_sum(packed, axis, ident)
    return [
        summed[start : start + piece.size // width].reshape(piece.shape)
        for piece, start in zip(pieces, starts)
    ]


def product(first_factor, second_factor, first_axis, second_axis):
    return lax.dot_general(
        first_factor,
        second_factor,
        (((first_axis,), (second_axis,)), ((), ())),
        preferred_element_type=jnp.float32,
    )


def head_mask(shape, head, head_size):
    lane = lax.broadcasted_iota(jnp.int32, shape, 1)
    return (lane >= head * head_size) & (lane < (head + 1) * head_size)


def attend_kernel(head_count, mixed, position, biases, out, weights, with_content, with_position):
    length = mixed.shape[0]
    width = out.shape[1]
    head_size = width // head_count
    queries = mixed[:, :width]
    keys = mixed[:, width : 2 * width].astype(jnp.bfloat16)
    values = mixed[:, 2 * width :].astype(jnp.bfloat16)
    with_content[...] = (queries + biases[0:1, :]).astype(jnp.bfloat16)
    with_position[...] = (queries + biases[1:2, :]).astype(jnp.bfloat16)
    attended = jnp.zeros((length, width), jnp.float32)
    for head in range(head_count):
        mask = head_mask((length, width), head, head_size)
        zero = jnp.zeros((length, width), jnp.bfloat16)
        content = product(jnp.where(mask, with_content[...], zero), keys, 1, 1)
        spread = product(jnp.where(mask, with_position[...], zero), position[...], 1, 1)
        relative = pltpu.roll(spread, length + 1, 1, stride=1, stride_axis=0)[:, :length]
        scores = (content + relative) * (1.0 / math.sqrt(head_size))
        top = jnp.max(scores, axis=1, keepdims=True)
        powers = jnp.exp(scores - top)
        share = (powers / jnp.sum(powers, axis=1, keepdims=True)).astype(jnp.bfloat16)
        weights[head] = share
        attended = jnp.where(mask, product(share, values, 1, 0), attended)
    out[...] = attended.astype(jnp.bfloat16)


def attend(mixed, position, biases, head_count):
    length = mixed.shape[0]
    width = mixed.shape[1] // 3
    flat = jax.ShapeDtypeStruct((length, width), jnp.bfloat16)
    return pl.pallas_call(
        functools.partial(attend_kernel, head_count),
        out_shape=(
            flat,
            jax.ShapeDtypeStruct((head_count, length, length), jnp.bfloat16),
            flat,
            flat,
        ),
        in_specs=[VMEM] * 3,
        out_specs=(VMEM,) * 4,
        compiler_params=pltpu.CompilerParams(vmem_limit_bytes=32 * 2**20),
        name="attend",
    )(mixed, position, biases)


def attend_back_kernel(
    head_count,
    grad_ref,
    mixed,
    reversed_position,
    weights,
    with_content,
    with_position,
    mixed_grad,
    position_grad,
    bias_grad,
):
    length, width = grad_ref.shape
    head_size = width // head_count
    row = lax.broadcasted_iota(jnp.int32, (length, length), 0)
    column = lax.broadcasted_iota(jnp.int32, (length, length), 1)
    flip = (row + column == length - 1).astype(jnp.float32).astype(jnp.bfloat16)
    zero = jnp.zeros((length, width), jnp.bfloat16)
    grad = grad_ref[...]
    keys = product(flip, mixed[:, width : 2 * width].astype(jnp.bfloat16), 1, 0).astype(jnp.bfloat16)
    values = product(flip, mixed[:, 2 * width :].astype(jnp.bfloat16), 1, 0).astype(jnp.bfloat16)
    value_grad = jnp.zeros((length, width), jnp.float32)
    key_grad = jnp.zeros((length, width), jnp.float32)
    content_grad = jnp.zeros((length, width), jnp.float32)
    spread_grad = jnp.zeros((length, width), jnp.float32)
    table_grad = jnp.zeros((2 * length, width), jnp.float32)
    for head in range(head_count):
        mask = head_mask((length, width), head, head_size)
        head_grad = jnp.where(mask, grad, zero)
        value_grad += product(weights[head], head_grad, 0, 0)
        share = product(weights[head], flip, 1, 0)
        share_grad = product(head_grad, values, 1, 1)
        inner = jnp.sum(share * share_grad, axis=1, keepdims=True)
        score_grad = (share * (share_grad - inner)).astype(jnp.bfloat16).astype(jnp.float32)
        score_grad = score_grad * (1.0 / math.sqrt(head_size))
        low_grad = score_grad.astype(jnp.bfloat16)
        content_grad = jnp.where(mask, product(low_grad, keys, 1, 0), content_grad)
        key_grad += product(low_grad, jnp.where(mask, with_content[...], zero), 0, 0)
        wide = jnp.concatenate([score_grad, jnp.zeros((length, length), jnp.float32)], axis=1)
        shifted = pltpu.roll(wide, 0, 1, stride=1, stride_axis=0).astype(jnp.bfloat16)
        spread_grad = jnp.where(mask, product(shifted, reversed_position[...], 1, 0), spread_grad)
        table_grad += product(shifted, jnp.where(mask, with_position[...], zero), 0, 0)
    mixed_grad[:, :width] = (content_grad + spread_grad).astype(jnp.bfloat16)
    mixed_grad[:, width : 2 * width] = product(flip, key_grad.astype(jnp.bfloat16), 1, 0).astype(
        jnp.bfloat16
    )
    mixed_grad[:, 2 * width :] = value_grad.astype(jnp.bfloat16)
    position_grad[...] = table_grad.astype(jnp.bfloat16)
    bias_grad[0:1, :] = jnp.sum(content_grad, axis=0, keepdims=True)
    bias_grad[1:2, :] = jnp.sum(spread_grad, axis=0, keepdims=True)


def attend_back(grad, mixed, reversed_position, kept, head_count):
    length, width = grad.shape
    return pl.pallas_call(
        functools.partial(attend_back_kernel, head_count),
        out_shape=(
            jax.ShapeDtypeStruct((length, 3 * width), jnp.bfloat16),
            jax.ShapeDtypeStruct((2 * length, width), jnp.bfloat16),
            jax.ShapeDtypeStruct((2, width), jnp.float32),
        ),
        in_specs=[VMEM] * 6,
        out_specs=(VMEM,) * 3,
        compiler_params=pltpu.CompilerParams(vmem_limit_bytes=32 * 2**20),
        name="attend_back",
    )(grad, mixed, reversed_position, *kept)


def halving_kernel(count, groups, part, out, work, land, send, recv):
    me = lax.axis_index("dp")
    bits = [1 << k for k in range(count.bit_length() - 1)]
    orders = [bits, bits[1:] + bits[:1]]
    stages = len(bits)
    height = part.shape[0] // groups
    barrier = pltpu.get_barrier_semaphore()

    def side(bit):
        return lax.rem(me // bit, 2)

    def partner(bit):
        return me + bit * (1 - 2 * side(bit))

    for bit in bits:
        pl.semaphore_signal(barrier, inc=1, device_id={"dp": partner(bit)}, device_id_type=MESH)
    pl.semaphore_wait(barrier, stages)

    def span(start, size):
        return pl.ds(pl.multiple_of(start, 8), size)

    spans = []
    for group in range(groups):
        start = group * height
        steps = []
        for k, bit in enumerate(orders[group % 2]):
            size = height >> (k + 1)
            keep = start + side(bit) * size
            give = start + (1 - side(bit)) * size
            steps.append((bit, span(keep, size), span(give, size)))
            start = keep
        spans.append(steps)

    def landing(group, k):
        return pl.ds(group * height + height - (height >> k), height >> (k + 1))

    def remote(source, target, group, stage, bit):
        return pltpu.make_async_remote_copy(
            src_ref=source,
            dst_ref=target,
            send_sem=send.at[group, stage],
            recv_sem=recv.at[group, stage],
            device_id={"dp": partner(bit)},
            device_id_type=MESH,
        )

    def down(group, k):
        bit, _, give = spans[group][k]
        source = part if k == 0 else work
        return remote(source.at[give], land.at[landing(group, k)], group, k, bit)

    def up(group, k):
        bit, keep, _ = spans[group][k]
        return remote(out.at[keep], out.at[keep], group, stages + k, bit)

    for group in range(groups):
        down(group, 0).start()
    for k in range(stages):
        for group in range(groups):
            keep = spans[group][k][1]
            source = part if k == 0 else work
            down(group, k).wait_recv()
            total = source[keep, :] + land[landing(group, k), :]
            if k < stages - 1:
                work[keep, :] = total
                down(group, k + 1).start()
            else:
                out[keep, :] = total
                up(group, k).start()
    for k in reversed(range(stages)):
        for group in range(groups):
            up(group, k).wait_recv()
            if k > 0:
                up(group, k - 1).start()
    for group in range(groups):
        for k in range(stages):
            down(group, k).wait_send()
            up(group, k).wait_send()


def halving_sum(part, ident, groups=4):
    count = lax.axis_size("dp")
    stages = count.bit_length() - 1
    buffer = pltpu.VMEM(part.shape, jnp.float32)
    return pl.pallas_call(
        functools.partial(halving_kernel, count, groups),
        out_shape=jax.ShapeDtypeStruct(part.shape, jnp.float32),
        in_specs=[VMEM],
        out_specs=VMEM,
        scratch_shapes=[
            buffer,
            buffer,
            pltpu.SemaphoreType.DMA((groups, 2 * stages)),
            pltpu.SemaphoreType.DMA((groups, 2 * stages)),
        ],
        compiler_params=pltpu.CompilerParams(
            collective_id=ident, has_side_effects=True, vmem_limit_bytes=32 * 2**20
        ),
        name="halving_sum",
    )(part)


def attention_front(values, gain_row, weight):
    normed = low(layer_norm(values, gain_row))
    return low_back(matmul(normed, weight))


def attention_back(attended, weight_out):
    return low_back(matmul(attended, weight_out))


def feed_forward(values, gain_row, weight_in, weight_out):
    normed = low(layer_norm(values, gain_row))
    hidden = low_back(matmul(normed, weight_in))
    active = low(jax.nn.silu(hidden))
    return low_back(matmul(active, weight_out))


def depthwise_conv(gated, kernel):
    half = kernel.shape[0] // 2
    return lax.conv_general_dilated(
        gated,
        kernel[:, None, :],
        (1,),
        [(half, half)],
        dimension_numbers=("NWC", "WIO", "NWC"),
        feature_group_count=gated.shape[2],
        precision=lax.Precision.HIGHEST,
    )


def conv_front(values, gain_row, weight_in, kernel):
    channels = kernel.shape[1]
    normed = low(layer_norm(values, gain_row))
    paired = low_back(matmul(normed, weight_in.reshape(weight_in.shape[0], 2 * channels))).reshape(
        -1, 2, channels
    )
    gated = paired[:, 0] * jax.nn.sigmoid(paired[:, 1])
    return depthwise_conv(gated.reshape(-1, LENGTH, channels), kernel)


def conv_back(mixed_rows, batch_mean, batch_var, scale_row, shift_row, weight_out):
    scaled = (mixed_rows - batch_mean) * lax.rsqrt(batch_var + EPS) * scale_row + shift_row
    swished = low(jax.nn.silu(scaled)).reshape(-1, mixed_rows.shape[2])
    return low_back(matmul(swished, weight_out))


def per_device(
    inputs,
    norm_gains,
    early_up,
    early_down,
    query_key_value,
    position_weight,
    position_bias,
    attention_out,
    pointwise_in,
    depthwise,
    batch_gain,
    batch_bias,
    pointwise_out,
    late_up,
    late_down,
    output_cotangent,
):
    stream = inputs.astype(jnp.float32)
    gain_rows = norm_gains.astype(jnp.float32)
    early_in = early_up.astype(jnp.float32)
    early_back = early_down.astype(jnp.float32)
    project_qkv = query_key_value.astype(jnp.float32)
    query_bias = position_bias.astype(jnp.float32)
    project_out = attention_out.astype(jnp.float32)
    point_first = pointwise_in.astype(jnp.float32)
    depth_taps = depthwise.astype(jnp.float32)
    scale_row = batch_gain.astype(jnp.float32)
    shift_row = batch_bias.astype(jnp.float32)
    point_second = pointwise_out.astype(jnp.float32)
    late_in = late_up.astype(jnp.float32)
    late_back = late_down.astype(jnp.float32)
    first_part, first_pull = jax.vjp(feed_forward, stream, gain_rows[0], early_in, early_back)
    after_first = tensor_sum(stream, first_part, 0.5, 0)

    model_width, _, local_width = project_qkv.shape
    head_count = query_bias.shape[1]
    table, reversed_table = sinusoid_tables(LENGTH, model_width)
    low_pos = position_weight
    position = product(table, low_pos, 1, 0).astype(jnp.bfloat16)
    reversed_position = product(reversed_table, low_pos, 1, 0).astype(jnp.bfloat16)
    bias_rows = query_bias.reshape(2, local_width)
    mixed_qkv, qkv_pull = jax.vjp(
        attention_front,
        after_first,
        gain_rows[1],
        project_qkv.reshape(model_width, 3 * local_width),
    )
    attended, *kept = attend(mixed_qkv, position, bias_rows, head_count)
    second_part, out_pull = jax.vjp(attention_back, attended.astype(jnp.float32), project_out)
    after_second = tensor_sum(after_first, second_part, 1.0, 1)
    mixed_rows, front_pull = jax.vjp(
        conv_front, after_second, gain_rows[2], point_first, depth_taps
    )
    token_count = mixed_rows.shape[0] * mixed_rows.shape[1] * lax.axis_size("dp")
    sum_values, sum_squares = exchange_many(
        (jnp.sum(mixed_rows, axis=(0, 1)), jnp.sum(mixed_rows * mixed_rows, axis=(0, 1))), "dp", 8
    )
    batch_mean = sum_values / token_count
    batch_var = sum_squares / token_count - batch_mean * batch_mean
    third_part, back_pull = jax.vjp(
        conv_back, mixed_rows, batch_mean, batch_var, scale_row, shift_row, point_second
    )
    after_third = tensor_sum(after_second, third_part, 1.0, 2)
    fourth_part, fourth_pull = jax.vjp(feed_forward, after_third, gain_rows[3], late_in, late_back)
    after_fourth = tensor_sum(after_third, fourth_part, 0.5, 3)
    result, final_pull = jax.vjp(layer_norm, after_fourth, gain_rows[4])
    grad_four, gain_five = final_pull(output_cotangent.astype(jnp.float32))
    cotangent_in, gain_four, late_in_grad, late_back_grad = fourth_pull(0.5 * grad_four)
    grad_three = tensor_sum(grad_four, cotangent_in, 1.0, 4)
    direct_grad, mean_grad, var_grad, scale_grad, shift_grad, second_point_grad = back_pull(
        grad_three
    )
    mean_grad, var_grad = exchange_many((mean_grad, var_grad), "dp", 9)
    mixed_grad = (
        direct_grad + (mean_grad + 2.0 * var_grad * (mixed_rows - batch_mean)) / token_count
    )
    cotangent_in, gain_three, first_point_grad, depth_grad = front_pull(mixed_grad)
    grad_two = tensor_sum(grad_three, cotangent_in, 1.0, 5)
    attended_grad, out_grad = out_pull(grad_two)
    late_in_grad, late_back_grad, second_point_grad, first_point_grad, out_grad = lax.psum(
        (
            late_in_grad,
            late_back_grad,
            second_point_grad,
            first_point_grad.reshape(model_width, 2 * local_width),
            out_grad,
        ),
        "dp",
    )
    qkv_grad, position_grad, bias_grad = attend_back(
        attended_grad.astype(jnp.bfloat16), mixed_qkv, reversed_position, kept, head_count
    )
    pos_grad = product(reversed_table, position_grad, 0, 0)
    cotangent_in, gain_two, qkv_grad = qkv_pull(qkv_grad.astype(jnp.float32))
    grad_one = tensor_sum(grad_two, cotangent_in, 1.0, 6)
    cotangent_in, gain_one, early_in_grad, early_back_grad = first_pull(0.5 * grad_one)
    pieces = (early_in_grad, early_back_grad, jnp.concatenate([qkv_grad, pos_grad], axis=1))
    summed = halving_sum(jnp.concatenate(pieces), 12, groups=3)
    early_in_grad, early_back_grad, middle_sum = jnp.split(summed, 3)
    grad_zero = tensor_sum(grad_one, cotangent_in, 1.0, 7)
    (gain_grads,) = exchange_many(
        (jnp.stack([gain_one, gain_two, gain_three, gain_four]),), "tensor", 10
    )
    gain_grads, gain_five, bias_grad, depth_grad, scale_grad, shift_grad = exchange_many(
        (gain_grads, gain_five, bias_grad, depth_grad, scale_grad, shift_grad), "dp", 11
    )
    return (
        result.astype(jnp.bfloat16),
        grad_zero,
        jnp.concatenate([gain_grads, gain_five[None]]),
        early_in_grad,
        early_back_grad,
        middle_sum[:, : 3 * local_width].reshape(query_key_value.shape),
        middle_sum[:, 3 * local_width :],
        bias_grad.reshape(position_bias.shape),
        out_grad,
        first_point_grad.reshape(pointwise_in.shape),
        depth_grad,
        scale_grad,
        shift_grad,
        second_point_grad,
        late_in_grad,
        late_back_grad,
    )


def solution(mesh):
    return jax.shard_map(
        per_device,
        mesh=mesh,
        in_specs=(
            P("dp", None),
            P(),
            P(None, "tensor"),
            P("tensor", None),
            P(None, None, "tensor"),
            P(None, "tensor"),
            P(None, "tensor", None),
            P("tensor", None),
            P(None, None, "tensor"),
            P(None, "tensor"),
            P("tensor"),
            P("tensor"),
            P("tensor", None),
            P(None, "tensor"),
            P("tensor", None),
            P("dp", None),
        ),
        out_specs=(
            P("dp", None),
            P("dp", None),
            P(),
            P(None, "tensor"),
            P("tensor", None),
            P(None, None, "tensor"),
            P(None, "tensor"),
            P(None, "tensor", None),
            P("tensor", None),
            P(None, None, "tensor"),
            P(None, "tensor"),
            P("tensor"),
            P("tensor"),
            P("tensor", None),
            P(None, "tensor"),
            P("tensor", None),
        ),
        check_vma=False,
    )
```
